32 devices in a mesh: band: 4 (over y, x), tile: 8 (over z, core).
Axes of the slice: x: 2, y: 2, z: 4, core: 2. Of those that a mesh axis runs over, the one named last changes fastest.
Arguments:
- image: float32 [432, 384, 512], P('band', 'tile'), may hold values from -60 to 60
Outputs:
- diffused: float32 [432, 384, 512], P('band', 'tile')
The draws below stay inside these ranges and needn't reach their ends.
All inputs are finite; a program needn't handle non-finite values.
Results may differ from the reference program's by a relative error of at most 0.0001.
Values sent between devices are 32-bit elements; how exact they have to be, the bound alone decides.
A program may use at most 128 MiB of HBM per device.

```python
import jax
import jax.numpy as jnp
from jax import lax

BANDS = 432
WIDTH = 512
ITERS = 3
HEIGHT = 384
N_BAND = 4


def draw_image(key, part):
    keys = jax.random.split(key, 4)
    band_pos = jnp.arange(BANDS).astype(jnp.float32) / max(BANDS - 1, 1)
    row_pos = jnp.arange(HEIGHT).astype(jnp.float32) / max(HEIGHT - 1, 1)
    gains = jnp.clip(jax.random.normal(keys[1], (BANDS, 1, 1), jnp.float32), -2.5, 2.5)
    jitter = jax.random.uniform(keys[3], (4,), jnp.float32, -0.3, 0.3)
    centres = (jnp.arange(4).astype(jnp.float32) + 0.5 + jitter) * 0.25
    closeness = (band_pos[:, None] - centres[None, :]) / 0.12
    affinity = jnp.exp(-closeness * closeness)
    total = affinity[:, 0] + affinity[:, 1] + affinity[:, 2] + affinity[:, 3]
    shares = affinity / total[:, None]
    sources = jnp.clip(jax.random.normal(keys[0], (4, HEIGHT, WIDTH), jnp.float32), -4.0, 4.0)
    noise = jnp.clip(jax.random.normal(keys[2], (BANDS, HEIGHT, WIDTH), jnp.float32), -4.0, 4.0)
    exponent = 0.5
    pattern = shares[:, 0, None, None] * sources[0][None, :, :]
    pattern = pattern + shares[:, 1, None, None] * sources[1][None, :, :]
    pattern = pattern + shares[:, 2, None, None] * sources[2][None, :, :]
    pattern = pattern + shares[:, 3, None, None] * sources[3][None, :, :]
    amplitude = (3.0 ** (exponent * band_pos))[:, None, None] * (3.0 ** (exponent * row_pos))[None, :, None]
    return amplitude * (0.8 * gains * pattern + 0.6 * noise)


def setup_inputs(seed: int = 0) -> dict:
    arg_keys = jax.random.split(jax.random.key(seed), 2)
    image = draw_image(jax.random.fold_in(arg_keys[1], 71), 0)
    return dict(image=image)


SMOOTH = (1.0 / 64.0, 6.0 / 64.0, 15.0 / 64.0, 20.0 / 64.0, 15.0 / 64.0, 6.0 / 64.0, 1.0 / 64.0)
STEP_SIZE = 0.25
KAPPA = 0.04
EPSILON = 1e-06

def gradients(block):
    padded = jnp.pad(block, ((0, 0), (1, 1), (1, 1)))
    grad_cols = (padded[:, 1:-1, 2:] - padded[:, 1:-1, :-2]) * 0.5
    grad_rows = (padded[:, 2:, 1:-1] - padded[:, :-2, 1:-1]) * 0.5
    return (grad_cols, grad_rows)

def smooth(field):
    height = field.shape[1]
    columns = field.shape[2]
    padded = jnp.pad(field, ((0, 0), (3, 3), (0, 0)))
    rowwise = sum((SMOOTH[k] * padded[:, k:k + height, :] for k in range(7)))
    padded = jnp.pad(rowwise, ((0, 0), (0, 0), (3, 3)))
    return sum((SMOOTH[k] * padded[:, :, k:k + columns] for k in range(7)))

def tensor_of(smoothed):
    s_xx, s_xy, s_yy = (smoothed[0], smoothed[1], smoothed[2])
    trace = s_xx + s_yy
    half = (s_xx - s_yy) * 0.5
    norm_value = jnp.sqrt(4.0 * half * half + 4.0 * s_xy * s_xy + KAPPA)
    f_minus = 1.0 / jnp.sqrt(1.0 + trace)
    f_plus = 1.0 / (1.0 + trace)
    mean_f = (f_minus + f_plus) * 0.5
    gap_f = f_plus - f_minus
    return (mean_f + gap_f * half / norm_value, gap_f * s_xy / norm_value, mean_f - gap_f * half / norm_value)

def update_of(block, t_xx, t_xy, t_yy):
    padded = jnp.pad(block, ((0, 0), (1, 1), (1, 1)))
    second_cols = padded[:, 1:-1, 2:] - 2.0 * block + padded[:, 1:-1, :-2]
    second_rows = padded[:, 2:, 1:-1] - 2.0 * block + padded[:, :-2, 1:-1]
    second_mixed = (padded[:, 2:, 2:] - padded[:, 2:, :-2] - padded[:, :-2, 2:] + padded[:, :-2, :-2]) * 0.25
    return t_xx * second_cols + 2.0 * t_xy * second_mixed + t_yy * second_rows

def reference(image):
    bands, height, columns = image.shape
    blocks = image.reshape(N_BAND, bands // N_BAND, height, columns)
    entries = float(bands * height * columns)
    for iteration in range(ITERS):

        def accumulate(carry, block):
            grad_cols, grad_rows = gradients(block)
            terms = jnp.stack([lax.optimization_barrier(jnp.sum(grad_cols * grad_cols, axis=0)), lax.optimization_barrier(jnp.sum(grad_cols * grad_rows, axis=0)), lax.optimization_barrier(jnp.sum(grad_rows * grad_rows, axis=0))])
            return (carry + terms, None)
        tensor, unused = lax.scan(accumulate, jnp.zeros((3, height, columns), jnp.float32), blocks)
        tensor = tensor / bands
        t_xx, t_xy, t_yy = tensor_of(smooth(tensor))
        updates = lax.map(lambda block: update_of(block, t_xx, t_xy, t_yy), blocks)
        energy = jnp.sum(updates * updates)
        step_value = STEP_SIZE / jnp.sqrt(energy / entries + EPSILON)
        blocks = blocks + step_value * updates
    return blocks.reshape(bands, height, columns)
```

```python
import functools

import jax
import jax.numpy as jnp
from jax import lax
from jax.experimental import pallas as pl
from jax.experimental.pallas import tpu as pltpu
from jax.sharding import PartitionSpec as P

ITERS = 3
LANES = 128
SMOOTH = (1.0 / 64.0, 6.0 / 64.0, 15.0 / 64.0, 20.0 / 64.0, 15.0 / 64.0, 6.0 / 64.0, 1.0 / 64.0)
STEP_SIZE = 0.25
KAPPA = 0.04
EPSILON = 1e-06


def shifted(pieces, lane, by):
    count = len(pieces)
    turned = [pltpu.roll(p, (-by) % LANES, 1) for p in pieces]
    edge = lane == (LANES - 1 if by == 1 else 0)
    zero = jnp.zeros_like(pieces[0])
    out = []
    for j in range(count):
        k = j + by
        out.append(jnp.where(edge, turned[k] if 0 <= k < count else zero, turned[j]))
    return out


def with_halo(cells, sides, width):
    for axis, dim in sides:
        count = lax.axis_size(axis)
        ends = count - 1
        head = lax.slice_in_dim(cells, 0, width, axis=dim)
        tail = lax.slice_in_dim(cells, cells.shape[dim] - width, cells.shape[dim], axis=dim)
        cells = jnp.concatenate(
            [
                lax.ppermute(tail, axis, [(i, (i + 1) % count) for i in range(ends)]),
                cells,
                lax.ppermute(head, axis, [((i + 1) % count, i) for i in range(ends)]),
            ],
            axis=dim,
        )
    return cells


def smooth_rows(field, rows):
    return sum((SMOOTH[k] * field[:, k : k + rows, :] for k in range(7)))


def smooth_columns(field):
    columns = field.shape[2]
    padded = jnp.pad(field, ((0, 0), (0, 0), (3, 3)))
    return sum((SMOOTH[k] * padded[:, :, k : k + columns] for k in range(7)))


def tensor_of(smoothed):
    s_xx, s_xy, s_yy = (smoothed[0], smoothed[1], smoothed[2])
    trace = s_xx + s_yy
    half = (s_xx - s_yy) * 0.5
    norm_value = jnp.sqrt(4.0 * half * half + 4.0 * s_xy * s_xy + KAPPA)
    f_minus = 1.0 / jnp.sqrt(1.0 + trace)
    f_plus = 1.0 / (1.0 + trace)
    mean_f = (f_minus + f_plus) * 0.5
    gap_f = f_plus - f_minus
    return (
        mean_f + gap_f * half / norm_value,
        gap_f * s_xy / norm_value,
        mean_f - gap_f * half / norm_value,
    )


def neighbours(above, prev, mid, nxt, below, b, n, NC):
    i = pl.program_id(0)
    last = pl.num_programs(0) - 1
    get = lambda ref: [ref[0, pl.ds(b, n), pl.ds(j * LANES, LANES)] for j in range(NC)]
    up = [jnp.where(i == 0, x, y) for x, y in zip(get(above), get(prev))]
    down = [jnp.where(i == last, x, y) for x, y in zip(get(below), get(nxt))]
    return up, get(mid), down


def tensor_kernel(above, prev, mid_ref, nxt, below, out):
    B, W = mid_ref.shape[1:]
    NC = W // LANES
    acc = {}
    for b in range(0, B, 8):
        n = min(8, B - b)
        lane = lax.broadcasted_iota(jnp.int32, (n, LANES), 1)
        up, mid, down = neighbours(above, prev, mid_ref, nxt, below, b, n, NC)
        right, left = shifted(mid, lane, 1), shifted(mid, lane, -1)
        for j in range(NC):
            gx, gy = right[j] - left[j], down[j] - up[j]
            for c, v in enumerate((gx * gx, gx * gy, gy * gy)):
                key = (n, c, j)
                acc[key] = acc[key] + v if key in acc else v
    for c in range(3):
        for j in range(NC):
            out[0, c:c + 1, pl.ds(j * LANES, LANES)] = sum(
                jnp.sum(acc[k], axis=0, keepdims=True) for k in sorted(acc) if k[1:] == (c, j))


def update_kernel(above, prev, mid_ref, nxt, below, coef, out, energy):
    B, W = mid_ref.shape[1:]
    NC = W // LANES
    w = [[jnp.broadcast_to(coef[0, k:k + 1, pl.ds(j * LANES, LANES)], (8, LANES))
          for j in range(NC)] for k in range(6)]
    acc = {}
    for b in range(0, B, 8):
        n = min(8, B - b)
        lane = lax.broadcasted_iota(jnp.int32, (n, LANES), 1)
        up, mid, down = neighbours(above, prev, mid_ref, nxt, below, b, n, NC)
        k = [[v[:n] for v in q] for q in w]
        g = [down[j] - up[j] for j in range(NC)]
        ahead = [k[0][j] * mid[j] + k[1][j] * g[j] for j in range(NC)]
        behind = [k[2][j] * mid[j] - k[3][j] * g[j] for j in range(NC)]
        ahead, behind = shifted(ahead, lane, 1), shifted(behind, lane, -1)
        for j in range(NC):
            u = (ahead[j] + behind[j]) + (k[4][j] * (down[j] + up[j]) + k[5][j] * mid[j])
            out[0, pl.ds(b, n), pl.ds(j * LANES, LANES)] = u
            acc[n, j] = acc[n, j] + u * u if (n, j) in acc else u * u
    energy[0] = sum(jnp.sum(v, axis=0, keepdims=True) for v in acc.values())


def per_device(image):
    B, rows, W = image.shape
    NB = lax.axis_size("band")
    nt = lax.axis_size("tile")
    bands = float(B * NB)
    entries = float(B * NB * rows * nt * W)
    one = lambda index: pl.BlockSpec((1, B, W), index)
    five = [one(lambda i: (0, 0, 0)), one(lambda i: (jnp.maximum(i - 1, 0), 0, 0)),
            one(lambda i: (i, 0, 0)), one(lambda i: (jnp.minimum(i + 1, rows - 1), 0, 0)),
            one(lambda i: (0, 0, 0))]
    line = lambda k, w: pl.BlockSpec((1, k, w), lambda i: (i, 0, 0))
    shape = lambda *s: jax.ShapeDtypeStruct(s, jnp.float32)
    params = pltpu.CompilerParams(vmem_limit_bytes=24 * 2**20)
    tensor = pl.pallas_call(tensor_kernel, grid=(rows,), in_specs=five, out_specs=line(3, W),
                            out_shape=shape(rows, 3, W), compiler_params=params, name="tensor")
    update = pl.pallas_call(update_kernel, grid=(rows,), in_specs=five + [line(6, W)],
                            out_specs=[line(B, W), line(1, LANES)],
                            out_shape=[shape(rows, B, W), shape(rows, 1, LANES)],
                            compiler_params=params, name="update")
    field = jnp.transpose(image, (1, 0, 2))
    down_pairs = [(i, i + 1) for i in range(nt - 1)]
    up_pairs = [(i + 1, i) for i in range(nt - 1)]
    ahead = lambda x: jnp.pad(x[:, 1:], ((0, 0), (0, 1)))
    behind = lambda x: jnp.pad(x[:, :-1], ((0, 0), (1, 0)))
    for _ in range(ITERS):
        above = lax.ppermute(field[rows - 1:], "tile", down_pairs)
        below = lax.ppermute(field[:1], "tile", up_pairs)
        part = tensor(above, field, field, field, below)
        part = jnp.transpose(part, (1, 0, 2))
        summed = lax.psum(part, "band") * (0.25 / bands)
        widened = with_halo(summed, (("tile", 1),), 3)
        t_xx, t_xy, t_yy = tensor_of(smooth_columns(smooth_rows(widened, rows)))
        t_xy = 0.5 * t_xy
        coef = jnp.stack([behind(t_xx), behind(t_xy), ahead(t_xx), ahead(t_xy), t_yy,
                          -2.0 * (t_xx + t_yy)], axis=1)
        change, energy = update(above, field, field, field, below, coef)
        total = lax.psum(jnp.sum(energy), ("band", "tile"))
        field = field + (STEP_SIZE / jnp.sqrt(total / entries + EPSILON)) * change
    return jnp.transpose(field, (1, 0, 2))


def solution(mesh):
    placed = (P("band", "tile", None),)
    return jax.shard_map(
        per_device, mesh=mesh, in_specs=placed, out_specs=P("band", "tile", None), check_vma=False
    )
```

```python
import functools

import jax
import jax.numpy as jnp
from jax import lax
from jax.experimental import pallas as pl
from jax.experimental.pallas import tpu as pltpu
from jax.sharding import PartitionSpec as P

ITERS = 3
LANES = 128
SMOOTH = (1.0 / 64.0, 6.0 / 64.0, 15.0 / 64.0, 20.0 / 64.0, 15.0 / 64.0, 6.0 / 64.0, 1.0 / 64.0)
STEP_SIZE = 0.25
KAPPA = 0.04
EPSILON = 1e-06


def shifted(pieces, lane, by):
    count = len(pieces)
    turned = [pltpu.roll(p, (-by) % LANES, 1) for p in pieces]
    edge = lane == (LANES - 1 if by == 1 else 0)
    zero = jnp.zeros_like(pieces[0])
    out = []
    for j in range(count):
        k = j + by
        out.append(jnp.where(edge, turned[k] if 0 <= k < count else zero, turned[j]))
    return out


def with_halo(cells, sides, width):
    for axis, dim in sides:
        count = lax.axis_size(axis)
        ends = count - 1
        head = lax.slice_in_dim(cells, 0, width, axis=dim)
        tail = lax.slice_in_dim(cells, cells.shape[dim] - width, cells.shape[dim], axis=dim)
        cells = jnp.concatenate(
            [
                lax.ppermute(tail, axis, [(i, (i + 1) % count) for i in range(ends)]),
                cells,
                lax.ppermute(head, axis, [((i + 1) % count, i) for i in range(ends)]),
            ],
            axis=dim,
        )
    return cells


def smooth_rows(field, rows):
    return sum((SMOOTH[k] * field[:, k : k + rows, :] for k in range(7)))


def smooth_columns(field):
    columns = field.shape[2]
    padded = jnp.pad(field, ((0, 0), (0, 0), (3, 3)))
    return sum((SMOOTH[k] * padded[:, :, k : k + columns] for k in range(7)))


def tensor_of(smoothed):
    s_xx, s_xy, s_yy = (smoothed[0], smoothed[1], smoothed[2])
    trace = s_xx + s_yy
    half = (s_xx - s_yy) * 0.5
    norm_value = jnp.sqrt(4.0 * half * half + 4.0 * s_xy * s_xy + KAPPA)
    f_minus = 1.0 / jnp.sqrt(1.0 + trace)
    f_plus = 1.0 / (1.0 + trace)
    mean_f = (f_minus + f_plus) * 0.5
    gap_f = f_plus - f_minus
    return (
        mean_f + gap_f * half / norm_value,
        gap_f * s_xy / norm_value,
        mean_f - gap_f * half / norm_value,
    )


def neighbours(above, prev, mid, nxt, below, b, n, NC):
    i = pl.program_id(0)
    last = pl.num_programs(0) - 1
    get = lambda ref: [ref[0, pl.ds(b, n), pl.ds(j * LANES, LANES)] for j in range(NC)]
    up = [jnp.where(i == 0, x, y) for x, y in zip(get(above), get(prev))]
    down = [jnp.where(i == last, x, y) for x, y in zip(get(below), get(nxt))]
    return up, get(mid), down


def tensor_kernel(above, prev, mid_ref, nxt, below, out):
    B, W = mid_ref.shape[1:]
    NC = W // LANES
    acc = {}
    for b in range(0, B, 8):
        n = min(8, B - b)
        lane = lax.broadcasted_iota(jnp.int32, (n, LANES), 1)
        up, mid, down = neighbours(above, prev, mid_ref, nxt, below, b, n, NC)
        right, left = shifted(mid, lane, 1), shifted(mid, lane, -1)
        for j in range(NC):
            gx, gy = right[j] - left[j], down[j] - up[j]
            for c, v in enumerate((gx * gx, gx * gy, gy * gy)):
                key = (n, c, j)
                acc[key] = acc[key] + v if key in acc else v
    for c in range(3):
        for j in range(NC):
            out[0, c:c + 1, pl.ds(j * LANES, LANES)] = sum(
                jnp.sum(acc[k], axis=0, keepdims=True) for k in sorted(acc) if k[1:] == (c, j))


def update_kernel(above, prev, mid_ref, nxt, below, coef, out, energy):
    B, W = mid_ref.shape[1:]
    NC = W // LANES
    w = [[jnp.broadcast_to(coef[0, k:k + 1, pl.ds(j * LANES, LANES)], (8, LANES))
          for j in range(NC)] for k in range(6)]
    acc = {}
    for b in range(0, B, 8):
        n = min(8, B - b)
        lane = lax.broadcasted_iota(jnp.int32, (n, LANES), 1)
        up, mid, down = neighbours(above, prev, mid_ref, nxt, below, b, n, NC)
        k = [[v[:n] for v in q] for q in w]
        g = [down[j] - up[j] for j in range(NC)]
        ahead = [k[0][j] * mid[j] + k[1][j] * g[j] for j in range(NC)]
        behind = [k[2][j] * mid[j] - k[3][j] * g[j] for j in range(NC)]
        ahead, behind = shifted(ahead, lane, 1), shifted(behind, lane, -1)
        for j in range(NC):
            u = (ahead[j] + behind[j]) + (k[4][j] * (down[j] + up[j]) + k[5][j] * mid[j])
            out[0, pl.ds(b, n), pl.ds(j * LANES, LANES)] = u
            acc[n, j] = acc[n, j] + u * u if (n, j) in acc else u * u
    energy[0] = sum(jnp.sum(v, axis=0, keepdims=True) for v in acc.values())


def total_over(x, axis):
    count = lax.axis_size(axis)
    if count & (count - 1):
        return lax.psum(x, axis)
    hop = 1
    while hop < count:
        x = x + lax.ppermute(x, axis, [(i, i ^ hop) for i in range(count)])
        hop *= 2
    return x


def per_device(image):
    B, rows, W = image.shape
    NB = lax.axis_size("band")
    nt = lax.axis_size("tile")
    bands = float(B * NB)
    entries = float(B * NB * rows * nt * W)
    one = lambda index: pl.BlockSpec((1, B, W), index)
    five = [one(lambda i: (0, 0, 0)), one(lambda i: (jnp.maximum(i - 1, 0), 0, 0)),
            one(lambda i: (i, 0, 0)), one(lambda i: (jnp.minimum(i + 1, rows - 1), 0, 0)),
            one(lambda i: (0, 0, 0))]
    line = lambda k, w: pl.BlockSpec((1, k, w), lambda i: (i, 0, 0))
    shape = lambda *s: jax.ShapeDtypeStruct(s, jnp.float32)
    params = pltpu.CompilerParams(vmem_limit_bytes=24 * 2**20)
    tensor = pl.pallas_call(tensor_kernel, grid=(rows,), in_specs=five, out_specs=line(3, W),
                            out_shape=shape(rows, 3, W), compiler_params=params, name="tensor")
    update = pl.pallas_call(update_kernel, grid=(rows,), in_specs=five + [line(6, W)],
                            out_specs=[line(B, W), line(1, LANES)],
                            out_shape=[shape(rows, B, W), shape(rows, 1, LANES)],
                            compiler_params=params, name="update")
    field = jnp.transpose(image, (1, 0, 2))
    down_pairs = [(i, i + 1) for i in range(nt - 1)]
    up_pairs = [(i + 1, i) for i in range(nt - 1)]
    ahead = lambda x: jnp.pad(x[:, 1:], ((0, 0), (0, 1)))
    behind = lambda x: jnp.pad(x[:, :-1], ((0, 0), (1, 0)))
    for _ in range(ITERS):
        above = lax.ppermute(field[rows - 1:], "tile", down_pairs)
        below = lax.ppermute(field[:1], "tile", up_pairs)
        part = tensor(above, field, field, field, below)
        part = jnp.transpose(part, (1, 0, 2))
        summed = total_over(part, "band") * (0.25 / bands)
        widened = with_halo(summed, (("tile", 1),), 3)
        t_xx, t_xy, t_yy = tensor_of(smooth_columns(smooth_rows(widened, rows)))
        t_xy = 0.5 * t_xy
        coef = jnp.stack([behind(t_xx), behind(t_xy), ahead(t_xx), ahead(t_xy), t_yy,
                          -2.0 * (t_xx + t_yy)], axis=1)
        change, energy = update(above, field, field, field, below, coef)
        total = total_over(total_over(jnp.sum(energy, axis=(0, 1)).reshape(1, LANES), "band"), "tile").sum()
        field = field + (STEP_SIZE / jnp.sqrt(total / entries + EPSILON)) * change
    return jnp.transpose(field, (1, 0, 2))


def solution(mesh):
    placed = (P("band", "tile", None),)
    return jax.shard_map(
        per_device, mesh=mesh, in_specs=placed, out_specs=P("band", "tile", None), check_vma=False
    )
```
